256 devices in a mesh: tile: 64 (over y, z, core), var: 4 (over x).
Axes of the slice: x: 4, y: 4, z: 8, core: 2. Of those that a mesh axis runs over, the one named last changes fastest.
Arguments:
- mesh_latents: bfloat16 [256, 262144], P('var', 'tile'), may hold values from -6 to 6
- edge_idx: int32 [3, 64, 8192], P(None, None, 'tile'), may hold values from 0 to 262143, as said below
- edge_weight: float32 [3, 64, 8192], P(None, None, 'tile'), may hold values from 0.2 to 1
- conv1_weight: bfloat16 [9, 512, 256], P(None, 'var'), may hold values from -0.125 to 0.125
- conv1_bias: float32 [512], P('var'), may hold values from -3 to 3
- conv2_weight: bfloat16 [9, 24, 512], P(None, None, 'var'), may hold values from -0.09375 to 0.09375
- conv2_bias: float32 [24], P('var'), may hold values from -3 to 3
Outputs:
- archive: float32 [24, 64, 8192], P('var', 'tile')
The draws below stay inside these ranges and needn't reach their ends.
Inputs may be any that keep to these rules, and one draw needn't show every extreme that they name: `edge_idx`: A grid cell in longitude column j has all three mesh nodes within 64 nodes, counted cyclically over 262144, of partition (j // 128), the nodes (j // 128) * 4096 to (j // 128 + 1) * 4096 - 1; the reach 64 is met on both sides.
All inputs are finite; a program needn't handle non-finite values.
Results may differ from the reference program's by a relative error of at most 0.0033.
Values may be sent and summed in bfloat16 or wider, within the bound.
No kernel may reach another device: no remote copies, remote signals or barrier semaphores. Data moves between devices by JAX's collectives and lax.ppermute only.
A program may use at most 320 MiB of HBM per device.

```python
import jax
import jax.numpy as jnp

LATENT = 256
HIDDEN_SIZE = 512
VARS = 24
LAT = 64
LON_DEV = 128
MESH_DEV = 4096
RIM = 64
NMESH = 262144
NLON = 8192


def draw_edge_idx(key, part):
    key = jax.random.fold_in(key, 11)
    column = jnp.arange(NLON, dtype=jnp.int32)
    stride = MESH_DEV // LON_DEV
    base = column // LON_DEV * MESH_DEV + column % LON_DEV * stride
    offset = jax.random.randint(key, (3, LAT, NLON), -RIM, RIM + stride, dtype=jnp.int32)
    return (base[None, None, :] + offset) % NMESH


def block_scale(rng, shape, cuts, least, top_value):
    def one(dim, blocks):
        steps = jax.random.uniform(jax.random.fold_in(jax.random.fold_in(rng, 6), dim), (blocks,), jnp.float32, least / len(cuts), top_value / len(cuts))
        return jnp.repeat(jnp.exp(steps), shape[dim] // blocks).reshape((-1,) + (1,) * (len(shape) - dim - 1))

    level = one(*cuts[0])
    for cut in cuts[1:]:
        level = level * one(*cut)
    return level


def normal_values(rng, extent, scale, most, cuts=(), kind=jnp.bfloat16):
    array = scale * jax.random.normal(rng, extent, jnp.float32)
    if cuts:
        array = array * block_scale(rng, extent, cuts, -0.22, 0.18)
    return jnp.clip(array, -most, most).astype(kind)


def setup_inputs(seed: int = 0) -> dict:
    streams_of = jax.random.split(jax.random.key(seed), 8)
    return {
        "mesh_latents": normal_values(streams_of[0], (LATENT, NMESH), 1.0, 6.0, ((0, 4), (1, 64))),
        "edge_idx": draw_edge_idx(jax.random.fold_in(streams_of[7], 71), 0),
        "edge_weight": jnp.clip(0.2 + 0.8 * jax.random.uniform(streams_of[2], (3, LAT, NLON), jnp.float32) ** block_scale(streams_of[2], (3, LAT, NLON), ((2, 64),), -0.2, 0.2), 0.2, 1.0),
        "conv1_weight": normal_values(streams_of[3], (9, HIDDEN_SIZE, LATENT), (9 * LATENT) ** -0.5, 0.125, ((1, 4),)),
        "conv1_bias": normal_values(streams_of[4], (HIDDEN_SIZE,), 0.5, 3.0, ((0, 4),), jnp.float32),
        "conv2_weight": normal_values(streams_of[5], (9, VARS, HIDDEN_SIZE), (9 * HIDDEN_SIZE) ** -0.5, 0.09375, ((2, 4),)),
        "conv2_bias": normal_values(streams_of[6], (VARS,), 0.5, 3.0, ((0, 4),), jnp.float32),
    }


def convolve(field, weight, bias):
    channels = field.shape[0]
    padded = jnp.pad(field, ((0, 0), (1, 1), (0, 0)))
    summed = jnp.zeros((weight.shape[1], LAT * NLON), jnp.float32)
    for row_off in range(3):
        for col_off in range(3):
            shifted = jnp.roll(padded[:, row_off:row_off + LAT, :], 1 - col_off, axis=2)
            summed = summed + jnp.dot(weight[3 * row_off + col_off].astype(jnp.float32),
                                      shifted.reshape(channels, LAT * NLON).astype(jnp.float32))
    return summed.reshape(weight.shape[1], LAT, NLON) + bias[:, None, None]


def reference(mesh_latents, edge_idx, edge_weight, conv1_weight, conv1_bias, conv2_weight, conv2_bias):
    gathered = jnp.zeros((LATENT, LAT, NLON), jnp.float32)
    for k in range(3):
        gathered = gathered + edge_weight[k] * jnp.take(mesh_latents, edge_idx[k], axis=1).astype(jnp.float32)
    decoded = gathered.astype(jnp.bfloat16)
    hidden = jax.nn.silu(convolve(decoded, conv1_weight, conv1_bias)).astype(jnp.bfloat16)
    return convolve(hidden, conv2_weight, conv2_bias)
```

```python
import jax
import jax.numpy as jnp
from jax import lax
from jax.experimental import pallas as pl
from jax.experimental.pallas import tpu as pltpu
from jax.sharding import PartitionSpec as P


GRP = 8


def prep(edge_idx, edge_weight, tile_at, mesh_dev, nmesh, rim):
    u = jnp.mod(edge_idx - tile_at * mesh_dev + rim, nmesh)
    u = u.transpose(0, 2, 1).reshape(3, -1, 128)
    wt = edge_weight.transpose(0, 2, 1).reshape(3, -1, 128)
    lo = jnp.min(u, axis=(0, 2)) // 64
    hi = jnp.max(u, axis=(0, 2)) // 64
    return u, wt, lo, hi

def decode_kernel(lo_ref, hi_ref, u_ref, wt_ref, lat_ref, left_ref, right_ref, out_ref, first_ref, last_ref, lats, parts, accs):
    ch, nodes = lat_ref.shape
    rim = left_ref.shape[1]
    ext = nodes + 2 * rim
    nblk = u_ref.shape[1]
    per = nblk // 4
    width = lats.shape[2]
    bf = lat_ref.dtype
    main = lat_ref[...]
    zeros = lambda n: jnp.zeros((ch, n), bf)
    lats[0] = jnp.concatenate([left_ref[...], main, right_ref[...], zeros(width - ext)], axis=1)
    lats[1] = jnp.concatenate([main, right_ref[...], zeros(width - ext + rim)], axis=1)

    u0, u1, u2 = u_ref[0], u_ref[1], u_ref[2]
    w0, w1, w2 = wt_ref[0], wt_ref[1], wt_ref[2]
    w0 = w0 + jnp.where(u1 == u0, w1, 0.0) + jnp.where(u2 == u0, w2, 0.0)
    w1 = w1 + jnp.where(u2 == u1, w2, 0.0)
    for k, w in enumerate((w0, w1, w2)):
        top = w.astype(bf).astype(jnp.float32)
        parts[k] = top
        parts[3 + k] = w - top

    node = lax.broadcasted_iota(jnp.int32, (256, 128), 0).astype(jnp.float32).astype(bf)

    def window(b, at):
        src = lats[at & 1, :, pl.ds(pl.multiple_of((at >> 1) * 128, 128), 256)]
        tops = jnp.zeros((256, 128), bf)
        rests = jnp.zeros((256, 128), bf)
        for k in (2, 1, 0):
            rel = (u_ref[k, pl.ds(b, 1), :] - at * 64).astype(jnp.float32).astype(bf)
            here = node == rel
            tops = jnp.where(here, parts[k, pl.ds(b, 1), :].astype(bf), tops)
            rests = jnp.where(here, parts[3 + k, pl.ds(b, 1), :].astype(bf), rests)
        table = jnp.concatenate([tops, rests], axis=1)
        both = jnp.dot(src, table, preferred_element_type=jnp.float32)
        return both[:, :128] + both[:, 128:]

    def group(g, _):
        more = jnp.int32(0)
        for j in range(GRP):
            b = g * GRP + j
            at = lo_ref[b]
            accs[j] = window(b, at)
            more = more + jnp.where(hi_ref[b] - at >= 4, 1, 0)

        @pl.when(more > 0)
        def _():
            for j in range(GRP):
                b = g * GRP + j
                at = lo_ref[b]

                @pl.loop(1, ((hi_ref[b] - at) >> 2) + 1)
                def _(step):
                    accs[j] += window(b, at + 4 * step)

        for j in range(GRP):
            b = g * GRP + j
            val = accs[j].astype(out_ref.dtype)
            piece, at = b // per, b % per
            out_ref[piece, :, pl.ds(pl.multiple_of(at * 128 + 128, 128), 128)] = val
            if j == 0:
                @pl.when(jnp.logical_and(at == 0, piece > 0))
                def _():
                    out_ref[piece - 1, :, (per + 1) * 128:] = val
                @pl.when(b == 0)
                def _():
                    first_ref[...] = val
            if j == GRP - 1:
                @pl.when(jnp.logical_and(at == per - 1, piece < 3))
                def _():
                    out_ref[piece + 1, :, :128] = val
                @pl.when(b == nblk - 1)
                def _():
                    last_ref[...] = val
        return 0
    lax.fori_loop(0, nblk // GRP, group, 0)
    out_ref[0, :, :128] = zeros(128)
    out_ref[3, :, (per + 1) * 128:] = zeros(128)

def decode(u, wt, lo, hi, lat, left, right):
    ch, nodes = lat.shape
    nblk = u.shape[1]
    smem = pl.BlockSpec(memory_space=pltpu.SMEM)
    vmem = pl.BlockSpec(memory_space=pltpu.VMEM)
    return pl.pallas_call(
        decode_kernel,
        out_shape=(
            jax.ShapeDtypeStruct((4, ch, (nblk // 4 + 2) * 128), lat.dtype),
            jax.ShapeDtypeStruct((ch, 128), lat.dtype),
            jax.ShapeDtypeStruct((ch, 128), lat.dtype),
        ),
        in_specs=[smem] * 2 + [vmem] * 5,
        out_specs=(vmem,) * 3,
        scratch_shapes=[pltpu.VMEM((2, ch, nodes + 384), lat.dtype), pltpu.VMEM((6, nblk, 128), jnp.float32), pltpu.VMEM((GRP, ch, 128), jnp.float32)],
        compiler_params=pltpu.CompilerParams(vmem_limit_bytes=40 << 20),
    )(lo, hi, u, wt, lat, left, right)


def conv_kernel(at_ref, grid_ref, h0, h1, h2, h3, *rest):
    weights = rest[:8]
    out_ref, shifted, mix, taps, rows = rest[8:]
    ch, cells = grid_ref.shape
    part = h0.shape[0]
    bf = grid_ref.dtype
    halos = (h0, h1, h2, h3)
    at = at_ref[0]
    lat = 64
    hid_cells = cells - 2 * lat
    out_cells = cells - 4 * lat

    place = lax.broadcasted_iota(jnp.int32, (1, cells), 1) % lat
    x = shifted
    x[1] = grid_ref[...]

    @pl.when(at == 0)
    def _():
        for d in range(4):
            s = (4 - d) % 4
            x[1, s * part:(s + 1) * part, :128] = halos[d][...]

    @pl.when(at == 3)
    def _():
        for d in range(4):
            s = 3 - d
            x[1, s * part:(s + 1) * part, cells - 128:] = halos[d][...]

    step = 64
    for c0 in range(0, ch, step):
        rs = slice(c0, c0 + step)
        v = x[1, rs, :].astype(jnp.float32)
        up = jnp.where(place == 0, 0.0, pltpu.roll(v, 1, 1))
        down = jnp.where(place == lat - 1, 0.0, pltpu.roll(v, cells - 1, 1))
        x[0, rs, :] = up.astype(bf)
        x[2, rs, :] = down.astype(bf)
        for r, u in enumerate((up, v, down)):
            x[3 + r, rs, :] = pltpu.roll(u, cells - lat, 1).astype(bf)

    last = jnp.concatenate([w[:, 9].reshape(64, 256) for w in weights], axis=0).astype(jnp.float32)
    mix[...] = last.T[:216].astype(bf)
    bias = last[:, 216:217] + last[:, 217:218] + last[:, 218:219]

    def tile(start, width):
        kernel_w = jnp.concatenate(
            [jnp.concatenate([w[:, k].reshape(64, 256) for w in weights], axis=0) for k in range(9)], axis=1)
        cols = []
        for r in range(3):
            for s in range(3):
                src, off = (3 + r, 0) if s == 1 else (r, s * lat)
                cols.append(x[src, :, pl.ds(start + off, width)])
        pre = jnp.dot(kernel_w, jnp.concatenate(cols, axis=0), preferred_element_type=jnp.float32) + bias
        hidden = pre * (0.5 * jnp.tanh(0.5 * pre) + 0.5)
        taps[:, pl.ds(start, width)] = jnp.dot(mix[...], hidden.astype(bf), preferred_element_type=jnp.float32)

    @pl.loop(0, hid_cells // 256)
    def _(n):
        tile(pl.multiple_of(n * 256, 256), 256)

    if hid_cells % 256:
        tile(hid_cells // 256 * 256, hid_cells % 256)

    def total(r):
        y = [taps[(3 * r + s) * 24:(3 * r + s + 1) * 24, :] for s in range(3)]
        mid = pltpu.roll(y[1], taps.shape[1] - lat, 1)
        return y[0][:, :out_cells] + mid[:, :out_cells] + y[2][:, 2 * lat:2 * lat + out_cells]

    spot = place[:, :out_cells]
    full = jnp.where(spot == 0, 0.0, pltpu.roll(total(0), 1, 1))
    full = full + total(1)
    full = full + jnp.where(spot == lat - 1, 0.0, pltpu.roll(total(2), out_cells - 1, 1))

    rows[...] = jnp.zeros_like(rows)
    for l in range(32):
        col = full[:, l * lat:(l + 1) * lat]
        for g in range(4):
            rows[pl.ds(g * 256 + l, 6, stride=32), :] = col[g * 6:g * 6 + 6]
    turned = rows[...].T
    for g in range(4):
        for h in range(2):
            out_ref[g * lat:(g + 1) * lat, h, :] = turned[:, g * 256 + h * 128:g * 256 + h * 128 + 128]

def convolve(at, grid, halos, weights):
    ch, cells = grid.shape
    smem = pl.BlockSpec(memory_space=pltpu.SMEM)
    vmem = pl.BlockSpec(memory_space=pltpu.VMEM)
    return pl.pallas_call(
        conv_kernel,
        out_shape=jax.ShapeDtypeStruct((256, 2, 128), jnp.float32),
        in_specs=[smem] + [vmem] * 13,
        out_specs=vmem,
        scratch_shapes=[
            pltpu.VMEM((6, ch, cells), grid.dtype),
            pltpu.VMEM((216, 512), grid.dtype),
            pltpu.VMEM((216, cells), jnp.float32),
            pltpu.VMEM((1024, 64), jnp.float32),
        ],
        compiler_params=pltpu.CompilerParams(vmem_limit_bytes=48 << 20),
    )(at, grid, *halos, *weights)
def finish_kernel(got_ref, bias_ref, out_ref):
    for k in range(6):
        half, lane = k // 4, k % 4 * 32
        out_ref[k] = jnp.concatenate(
            [got_ref[64 * v:64 * v + 64, half, lane:lane + 32] for v in range(4)], axis=1) + bias_ref[k]

def finish(got, bias):
    smem = pl.BlockSpec(memory_space=pltpu.SMEM)
    vmem = pl.BlockSpec(memory_space=pltpu.VMEM)
    return pl.pallas_call(
        finish_kernel,
        out_shape=jax.ShapeDtypeStruct((6, 64, 128), jnp.float32),
        in_specs=[vmem, smem],
        out_specs=vmem,
    )(got, bias)


def gathered_weights(conv1_weight, conv1_bias, conv2_weight):
    tile_at = lax.axis_index("tile")
    share = 2 * (tile_at // 16) + tile_at % 2
    first = lax.dynamic_slice_in_dim(conv1_weight, 16 * share, 16, 1)
    second = lax.dynamic_slice_in_dim(conv2_weight, 16 * share, 16, 2).reshape(216, 16).T
    bias = lax.dynamic_slice_in_dim(conv1_bias, 16 * share, 16, 0)
    terms = []
    for _ in range(3):
        term = lax.reduce_precision(bias, 8, 7)
        bias = bias - term
        terms.append(term.astype(jnp.bfloat16)[:, None])
    rest = jnp.pad(jnp.concatenate([second] + terms, axis=1), ((0, 0), (0, 37)))
    mine = jnp.concatenate([first, rest[None]], axis=0)
    var_count, tiles = lax.axis_size("var"), lax.axis_size("tile")
    parts = [mine]
    for d in range(1, var_count):
        parts.append(lax.ppermute(mine, "var", [(i, (i + d) % var_count) for i in range(var_count)]))
    column = jnp.stack(parts)
    blocks = [column]
    for e in range(1, 4):
        blocks.append(lax.ppermute(column, "tile", [(i, (i + 16 * e) % tiles) for i in range(tiles)]))
    swap = [(i, i ^ 1) for i in range(tiles)]
    return blocks + [lax.ppermute(b, "tile", swap) for b in blocks]


def body(mesh_latents, edge_idx, edge_weight, conv1_weight, conv1_bias, conv2_weight, conv2_bias):
    tile_at, var_at = lax.axis_index("tile"), lax.axis_index("var")
    tiles, var_count = lax.axis_size("tile"), lax.axis_size("var")
    mesh_dev = mesh_latents.shape[1]
    rim = 64
    up = [(i, (i + 1) % tiles) for i in range(tiles)]
    down = [(j, i) for i, j in up]
    left = lax.ppermute(mesh_latents[:, mesh_dev - rim:], "tile", up)
    right = lax.ppermute(mesh_latents[:, :rim], "tile", down)
    u, wt, lo, hi = prep(edge_idx, edge_weight, tile_at, mesh_dev, mesh_dev * tiles, rim)
    pieces, first, last = decode(u, wt, lo, hi, mesh_latents, left, right)

    halos = []
    for d in range(4):
        to_first = [(4 * t + (4 - d) % 4, (t + 1) % tiles * 4) for t in range(tiles)]
        to_last = [(4 * t + 3 - d, (t - 1) % tiles * 4 + 3) for t in range(tiles)]
        edge = jnp.where(var_at == (4 - d) % 4, last, first)
        halos.append(lax.ppermute(edge, ("tile", "var"), to_first + to_last))

    weights = gathered_weights(conv1_weight, conv1_bias, conv2_weight)
    grid = lax.all_to_all(pieces, "var", split_axis=0, concat_axis=0, tiled=True)
    grid = grid.reshape(grid.shape[0] * grid.shape[1], grid.shape[2])
    fields = convolve(var_at.reshape(1), grid, halos, weights)
    got = lax.all_to_all(fields, ("var", "tile"), split_axis=0, concat_axis=0, tiled=True)
    return finish(got, conv2_bias).reshape(6, 1, tiles * 128)


def solution(mesh):
    return jax.shard_map(
        body,
        mesh=mesh,
        in_specs=(
            P("var", "tile"),
            P(None, None, "tile"),
            P(None, None, "tile"),
            P(None, "var", None),
            P("var"),
            P(None, None, "var"),
            P("var"),
        ),
        out_specs=P("var", "tile", None),
        check_vma=False,
    )
```

```python
import functools

import jax
import jax.numpy as jnp
from jax import lax
from jax.experimental import pallas as pl
from jax.experimental.pallas import tpu as pltpu
from jax.sharding import PartitionSpec as P


GRP = 8
TILE = 2304


def prep(edge_idx, edge_weight, tile_at, mesh_dev, nmesh, rim):
    u = jnp.mod(edge_idx - tile_at * mesh_dev + rim, nmesh)
    u = u.transpose(0, 2, 1).reshape(3, -1, 128)
    wt = edge_weight.transpose(0, 2, 1).reshape(3, -1, 128)
    lo = jnp.min(u, axis=(0, 2)) // 64
    hi = jnp.max(u, axis=(0, 2)) // 64
    return u, wt, lo, hi

def decode_kernel(blocks, lo_ref, hi_ref, u_ref, wt_ref, lat_ref, left_ref, right_ref, *rest):
    outs, (lats, parts, accs) = rest[:-3], rest[-3:]
    ch, nodes = lat_ref.shape
    rim = left_ref.shape[1]
    ext = nodes + 2 * rim
    nblk = u_ref.shape[1]
    width = lats.shape[2]
    bf = lat_ref.dtype
    main = lat_ref[...]
    zeros = lambda n: jnp.zeros((ch, n), bf)
    lats[0] = jnp.concatenate([left_ref[...], main, right_ref[...], zeros(width - ext)], axis=1)
    lats[1] = jnp.concatenate([main, right_ref[...], zeros(width - ext + rim)], axis=1)

    u0, u1, u2 = u_ref[0], u_ref[1], u_ref[2]
    w0, w1, w2 = wt_ref[0], wt_ref[1], wt_ref[2]
    w0 = w0 + jnp.where(u1 == u0, w1, 0.0) + jnp.where(u2 == u0, w2, 0.0)
    w1 = w1 + jnp.where(u2 == u1, w2, 0.0)
    for k, w in enumerate((w0, w1, w2)):
        top = w.astype(bf).astype(jnp.float32)
        parts[k] = top
        parts[3 + k] = w - top

    node = lax.broadcasted_iota(jnp.int32, (256, 128), 0).astype(jnp.float32).astype(bf)

    def window(b, at):
        src = lats[at & 1, :, pl.ds(pl.multiple_of((at >> 1) * 128, 128), 256)]
        tops = jnp.zeros((256, 128), bf)
        rests = jnp.zeros((256, 128), bf)
        for k in (2, 1, 0):
            rel = (u_ref[k, pl.ds(b, 1), :] - at * 64).astype(jnp.float32).astype(bf)
            here = node == rel
            tops = jnp.where(here, parts[k, pl.ds(b, 1), :].astype(bf), tops)
            rests = jnp.where(here, parts[3 + k, pl.ds(b, 1), :].astype(bf), rests)
        table = jnp.concatenate([tops, rests], axis=1)
        both = jnp.dot(src, table, preferred_element_type=jnp.float32)
        return both[:, :128] + both[:, 128:]

    def several(ids):
        more = jnp.int32(0)
        for j, b in enumerate(ids):
            at = lo_ref[b]
            accs[j] = window(b, at)
            more = more + jnp.where(hi_ref[b] - at >= 4, 1, 0)

        @pl.when(more > 0)
        def _():
            for j, b in enumerate(ids):
                at = lo_ref[b]

                @pl.loop(1, ((hi_ref[b] - at) >> 2) + 1)
                def _(step):
                    accs[j] += window(b, at + 4 * step)

    if blocks is not None:
        several(blocks)
        for j, out in enumerate(outs):
            out[...] = accs[j].astype(out.dtype)
        return

    out_ref, = outs
    per = nblk // 4

    def group(g, _):
        several([g * GRP + j for j in range(GRP)])
        for j in range(GRP):
            b = g * GRP + j
            val = accs[j].astype(out_ref.dtype)
            piece, at = b // per, b % per
            out_ref[piece, :, pl.ds(pl.multiple_of(at * 128 + 128, 128), 128)] = val
            if j == 0:
                @pl.when(jnp.logical_and(at == 0, piece > 0))
                def _():
                    out_ref[piece - 1, :, (per + 1) * 128:] = val
            if j == GRP - 1:
                @pl.when(jnp.logical_and(at == per - 1, piece < 3))
                def _():
                    out_ref[piece + 1, :, :128] = val
        return 0
    lax.fori_loop(0, nblk // GRP, group, 0)


def decode(u, wt, lo, hi, lat, left, right, blocks=None):
    ch, nodes = lat.shape
    nblk = u.shape[1]
    smem = pl.BlockSpec(memory_space=pltpu.SMEM)
    vmem = pl.BlockSpec(memory_space=pltpu.VMEM)
    if blocks is None:
        shapes, done = (jax.ShapeDtypeStruct((4, ch, (nblk // 4 + 2) * 128), lat.dtype),), nblk
    else:
        shapes, done = (jax.ShapeDtypeStruct((ch, 128), lat.dtype),) * len(blocks), len(blocks)
    return pl.pallas_call(
        functools.partial(decode_kernel, blocks),
        out_shape=shapes,
        in_specs=[smem] * 2 + [vmem] * 5,
        out_specs=(vmem,) * len(shapes),
        scratch_shapes=[
            pltpu.VMEM((2, ch, nodes + 384), lat.dtype),
            pltpu.VMEM((6, nblk, 128), jnp.float32),
            pltpu.VMEM((GRP, ch, 128), jnp.float32),
        ],
        cost_estimate=pl.CostEstimate(flops=done * 256 * 128 * 4 * ch * 16, bytes_accessed=2 * ch * nodes * 2, transcendentals=0),
        compiler_params=pltpu.CompilerParams(vmem_limit_bytes=24 << 20),
    )(lo, hi, u, wt, lat, left, right)


def conv_kernel(var_ref, grid_ref, *rest):
    sources = rest[:8]
    out_ref, wts, shifted, mix, taps, rows, pairs, sems = rest[8:]
    copies = [pltpu.make_async_copy(src, wts.at[g], sems.at[g]) for g, src in enumerate(sources)]
    for copy in copies:
        copy.start()
    ch, cells = grid_ref.shape
    bf = grid_ref.dtype
    lat = 64
    out_cells = cells - 4 * lat

    place = lax.broadcasted_iota(jnp.int32, (1, cells), 1) % lat
    x = shifted
    x[1, :, :cells] = grid_ref[...]

    x[:, :, cells:] = jnp.zeros((6, ch, 128), bf)
    step = 64
    for c0 in range(0, ch, step):
        rs = slice(c0, c0 + step)
        v = grid_ref[rs, :].astype(jnp.float32)
        up = jnp.where(place == 0, 0.0, pltpu.roll(v, 1, 1))
        down = jnp.where(place == lat - 1, 0.0, pltpu.roll(v, cells - 1, 1))
        x[0, rs, :cells] = up.astype(bf)
        x[2, rs, :cells] = down.astype(bf)
        for r, u in enumerate((up, v, down)):
            x[3 + r, rs, :cells] = pltpu.roll(u, cells - lat, 1).astype(bf)

    for copy in copies:
        copy.wait()
    weights = [wts.at[g] for g in range(8)]

    last = jnp.concatenate([w[9] for w in weights], axis=0).astype(jnp.float32)
    mix[...] = last.T[:216].astype(bf)
    bias = last[:, 216:217] + last[:, 217:218] + last[:, 218:219]

    def tile(start, width):
        kernel_w = jnp.concatenate(
            [jnp.concatenate([w[k] for w in weights], axis=0) for k in range(9)], axis=1)
        cols = []
        for r in range(3):
            for s in range(3):
                src, off = (3 + r, 0) if s == 1 else (r, s * lat)
                cols.append(x[src, :, pl.ds(start + off, width)])
        pre = jnp.dot(kernel_w, jnp.concatenate(cols, axis=0), preferred_element_type=jnp.float32) + bias
        hidden = pre * (0.5 * jnp.tanh(0.5 * pre) + 0.5)
        taps[:, pl.ds(start, width)] = jnp.dot(mix[...], hidden.astype(bf), preferred_element_type=jnp.float32)

    @pl.loop(0, cells // TILE)
    def _(n):
        tile(pl.multiple_of(n * TILE, 128), TILE)

    def total(r):
        y = [taps[(3 * r + s) * 24:(3 * r + s + 1) * 24, :] for s in range(3)]
        mid = pltpu.roll(y[1], taps.shape[1] - lat, 1)
        return y[0][:, :out_cells] + mid[:, :out_cells] + y[2][:, 2 * lat:2 * lat + out_cells]

    spot = place[:, :out_cells]
    full = jnp.where(spot == 0, 0.0, pltpu.roll(total(0), 1, 1))
    full = full + total(1)
    full = full + jnp.where(spot == lat - 1, 0.0, pltpu.roll(total(2), out_cells - 1, 1))

    shift = []
    for g in range(4):
        terms = wts[(var_ref[0] - g) & 3, 9, 0:16, :].astype(jnp.float32)[:6]
        shift.append(terms[:, 219:220] + terms[:, 220:221] + terms[:, 221:222])
    full = full + jnp.concatenate(shift, axis=0)

    rows[...] = jnp.zeros_like(rows)
    for l in range(32):
        col = full[:, l * lat:(l + 1) * lat]
        for g in range(4):
            rows[pl.ds(g * 256 + l, 6, stride=32), :] = col[g * 6:g * 6 + 6]
    turned = rows[...].T
    for g in range(4):
        for h in range(2):
            pairs[pl.ds(g * 2 * lat + h, lat, stride=2), :] = turned[:, g * 256 + h * 128:g * 256 + h * 128 + 128]
    out_ref[...] = pairs[...].astype(out_ref.dtype)

def convolve(var_at, grid, weights):
    ch, cells = grid.shape
    vmem = pl.BlockSpec(memory_space=pltpu.VMEM)
    return pl.pallas_call(
        conv_kernel,
        out_shape=jax.ShapeDtypeStruct((512, 128), grid.dtype),
        in_specs=[pl.BlockSpec(memory_space=pltpu.SMEM), vmem] + [pl.BlockSpec(memory_space=pltpu.HBM)] * 8,
        out_specs=vmem,
        scratch_shapes=[
            pltpu.VMEM((8,) + weights[0].shape, grid.dtype),
            pltpu.VMEM((6, ch, cells + 128), grid.dtype),
            pltpu.VMEM((216, 512), grid.dtype),
            pltpu.VMEM((216, cells), jnp.float32),
            pltpu.VMEM((1024, 64), jnp.float32),
            pltpu.VMEM((512, 128), jnp.float32),
            pltpu.SemaphoreType.DMA((8,)),
        ],
        compiler_params=pltpu.CompilerParams(vmem_limit_bytes=24 << 20),
    )(var_at, grid, *weights)
def finish_kernel(got_ref, out_ref, pairs):
    pairs[...] = got_ref[...].astype(jnp.float32)
    for k in range(6):
        half, lane = k // 4, k % 4 * 32
        out_ref[k] = jnp.concatenate(
            [pairs[pl.ds(128 * v + half, 64, stride=2), :][:, lane:lane + 32] for v in range(4)], axis=1)


def finish(got):
    vmem = pl.BlockSpec(memory_space=pltpu.VMEM)
    return pl.pallas_call(
        finish_kernel,
        out_shape=jax.ShapeDtypeStruct((6, 64, 128), jnp.float32),
        in_specs=[vmem],
        out_specs=vmem,
        scratch_shapes=[pltpu.VMEM((512, 128), jnp.float32)],
    )(got)


def bf16_terms(value):
    terms = []
    for _ in range(3):
        term = lax.reduce_precision(value, 8, 7)
        value = value - term
        terms.append(term.astype(jnp.bfloat16)[:, None])
    return terms


def gathered_weights(conv1_weight, conv1_bias, conv2_weight, conv2_bias):
    tile_at = lax.axis_index("tile")
    half = conv1_weight.shape[1] // 2
    start = half * (tile_at % 2)
    first = lax.dynamic_slice_in_dim(conv1_weight, start, half, 1)
    second = lax.dynamic_slice_in_dim(conv2_weight, start, half, 2).reshape(216, half).T
    bias = lax.dynamic_slice_in_dim(conv1_bias, start, half, 0)
    terms = bf16_terms(bias)
    terms += [jnp.pad(t, ((0, half - t.shape[0]), (0, 0))) for t in bf16_terms(conv2_bias)]
    rest = jnp.pad(jnp.concatenate([second] + terms, axis=1), ((0, 0), (0, 34)))
    mine = jnp.concatenate([first, rest[None]], axis=0)
    count = lax.axis_size("var")
    return [mine] + [lax.ppermute(mine, "var", [(i, (i + d) % count) for i in range(count)]) for d in range(1, count)]


def exchanged_weights(blocks):
    tiles = lax.axis_size("tile")
    return blocks + [lax.ppermute(b, "tile", [(i, i ^ 1) for i in range(tiles)]) for b in blocks]


def body(mesh_latents, edge_idx, edge_weight, conv1_weight, conv1_bias, conv2_weight, conv2_bias):
    tile_at = lax.axis_index("tile")
    tiles = lax.axis_size("tile")
    mesh_dev = mesh_latents.shape[1]
    rim = 64
    up = [(i, (i + 1) % tiles) for i in range(tiles)]
    down = [(j, i) for i, j in up]
    left = lax.ppermute(mesh_latents[:, mesh_dev - rim:], "tile", up)
    right = lax.ppermute(mesh_latents[:, :rim], "tile", down)
    blocks = gathered_weights(conv1_weight, conv1_bias, conv2_weight, conv2_bias)
    u, wt, lo, hi = prep(edge_idx, edge_weight, tile_at, mesh_dev, mesh_dev * tiles, rim)
    first, last = decode(u, wt, lo, hi, mesh_latents, left, right, (0, u.shape[1] - 1))
    before = lax.ppermute(last, "tile", up)
    after = lax.ppermute(first, "tile", down)
    pieces, = decode(u, wt, lo, hi, mesh_latents, left, right)
    pieces = lax.dynamic_update_slice(pieces, before[None], (0, 0, 0))
    pieces = lax.dynamic_update_slice(pieces, after[None], (3, 0, pieces.shape[2] - 128))

    pieces, blocks = lax.optimization_barrier((pieces, blocks))
    weights = exchanged_weights(blocks)
    grid = lax.all_to_all(pieces, "var", split_axis=0, concat_axis=0, tiled=True)
    grid = grid.reshape(grid.shape[0] * grid.shape[1], grid.shape[2])
    fields = convolve(lax.axis_index("var").reshape(1), grid, weights)
    got = lax.all_to_all(fields.reshape(256, 2, 128), ("var", "tile"), split_axis=0, concat_axis=0, tiled=True)
    return finish(got.reshape(512, 128)).reshape(6, 1, tiles * 128)


def solution(mesh):
    return jax.shard_map(
        body,
        mesh=mesh,
        in_specs=(
            P("var", "tile"),
            P(None, None, "tile"),
            P(None, None, "tile"),
            P(None, "var", None),
            P("var"),
            P(None, None, "var"),
            P("var"),
        ),
        out_specs=P("var", "tile", None),
        check_vma=False,
    )
```

```python
import functools

import jax
import jax.numpy as jnp
from jax import lax
from jax.experimental import pallas as pl
from jax.experimental.pallas import tpu as pltpu
from jax.sharding import PartitionSpec as P


def prep(edge_idx, edge_weight, tile_at, mesh_dev, nmesh, rim):
    u = jnp.mod(edge_idx - tile_at * mesh_dev + rim, nmesh)
    u = u.transpose(0, 2, 1).reshape(3, -1, 128)
    wt = edge_weight.transpose(0, 2, 1).reshape(3, -1, 128)
    lo = jnp.min(u, axis=(0, 2)) // 64
    hi = jnp.max(u, axis=(0, 2)) // 64
    return u, wt, lo, hi

LIMIT = 16


def decode_kernel(part, at_ref, lo_ref, hi_ref, u_ref, wt_ref, lat_ref, near_ref, far_ref, *rest):
    even = at_ref[1] == 0
    sides = lambda near, far: (jnp.where(even, far, near), jnp.where(even, near, far))
    left, right = sides(near_ref[...], far_ref[...])
    if part == "outer":
        near_out_ref, far_out_ref, *rest = rest
        before, after = sides(near_out_ref[...], far_out_ref[...])
    outs, (lats, parts, accs) = rest[:-3], rest[-3:]
    ch, nodes = lat_ref.shape
    rim = near_ref.shape[1]
    ext = nodes + 2 * rim
    nblk = u_ref.shape[1]
    width = lats.shape[2]
    bf = lat_ref.dtype
    main = lat_ref[...]
    zeros = lambda n: jnp.zeros((ch, n), bf)
    lats[0] = jnp.concatenate([left, main, right, zeros(width - ext)], axis=1)
    lats[1] = jnp.concatenate([main, right, zeros(width - ext + rim)], axis=1)

    u0, u1, u2 = u_ref[0], u_ref[1], u_ref[2]
    w0, w1, w2 = wt_ref[0], wt_ref[1], wt_ref[2]
    w0 = w0 + jnp.where(u1 == u0, w1, 0.0) + jnp.where(u2 == u0, w2, 0.0)
    w1 = w1 + jnp.where(u2 == u1, w2, 0.0)
    for k, w in enumerate((w0, w1, w2)):
        top = w.astype(bf).astype(jnp.float32)
        parts[k] = top
        parts[3 + k] = w - top

    node = lax.broadcasted_iota(jnp.int32, (256, 128), 0).astype(jnp.float32).astype(bf)

    def window(b, at):
        src = lats[at & 1, :, pl.ds(pl.multiple_of((at >> 1) * 128, 128), 256)]
        tops = jnp.zeros((256, 128), bf)
        rests = jnp.zeros((256, 128), bf)
        for k in (2, 1, 0):
            rel = (u_ref[k, pl.ds(b, 1), :] - at * 64).astype(jnp.float32).astype(bf)
            here = node == rel
            tops = jnp.where(here, parts[k, pl.ds(b, 1), :].astype(bf), tops)
            rests = jnp.where(here, parts[3 + k, pl.ds(b, 1), :].astype(bf), rests)
        table = jnp.concatenate([tops, rests], axis=1)
        both = jnp.dot(src, table, preferred_element_type=jnp.float32)
        return both[:, :128] + both[:, 128:]

    def several(ids):
        more = jnp.int32(0)
        for j, b in enumerate(ids):
            at = lo_ref[b]
            accs[j] = window(b, at)
            more = more + jnp.where(hi_ref[b] - at >= 4, 1, 0)

        @pl.when(more > 0)
        def _():
            for j, b in enumerate(ids):
                at = lo_ref[b]

                @pl.loop(1, ((hi_ref[b] - at) >> 2) + 1)
                def _(step):
                    accs[j] += window(b, at + 4 * step)

    if part == "edges":
        several((0, nblk - 1))
        first, last = accs[0].astype(bf), accs[1].astype(bf)
        outs[0][...] = jnp.where(even, last, first)
        outs[1][...] = jnp.where(even, first, last)
        return

    per = nblk // 4
    inner = per // 2 + 1
    outer = per + 1 - inner
    for d in range(4):
        v = (at_ref[0] + d) & 3
        if part == "inner":
            several([v * per + j for j in range(inner)])
            for j in range(inner):
                outs[0][v, :, j * 128:j * 128 + 128] = accs[j].astype(bf)
            continue
        several([jnp.minimum(v * per + inner + j, nblk - 1) for j in range(outer)])
        for j in range(outer - 1):
            outs[d][:, j * 128 + 128:j * 128 + 256] = accs[j].astype(bf)
        outs[d][:, outer * 128:] = jnp.where(v == 3, after, accs[outer - 1].astype(bf))
        outs[(d + 1) % 4][:, :128] = jnp.where(v == 3, before, accs[outer - 2].astype(bf))


def decode(part, at, u, wt, lo, hi, lat, near, far, *halos):
    ch, nodes = lat.shape
    nblk = u.shape[1]
    smem = pl.BlockSpec(memory_space=pltpu.SMEM)
    vmem = pl.BlockSpec(memory_space=pltpu.VMEM)
    group = nblk // 8 + 1
    if part == "edges":
        shapes, done = (jax.ShapeDtypeStruct((ch, 128), lat.dtype),) * 2, 2
    elif part == "inner":
        shapes, done = (jax.ShapeDtypeStruct((4, ch, group * 128), lat.dtype),), nblk // 2
    else:
        shapes, done = (jax.ShapeDtypeStruct((ch, group * 128), lat.dtype),) * 4, nblk // 2
    return pl.pallas_call(
        functools.partial(decode_kernel, part),
        out_shape=shapes,
        in_specs=[smem] * 3 + [vmem] * (5 + len(halos)),
        out_specs=(vmem,) * len(shapes),
        scratch_shapes=[
            pltpu.VMEM((2, ch, nodes + 384), lat.dtype),
            pltpu.VMEM((6, nblk, 128), jnp.float32),
            pltpu.VMEM((group, ch, 128), jnp.float32),
        ],
        cost_estimate=pl.CostEstimate(flops=done * 256 * 128 * 4 * ch * 16, bytes_accessed=2 * ch * nodes * 2, transcendentals=0),
        compiler_params=pltpu.CompilerParams(vmem_limit_bytes=8 << 20),
    )(at, lo, hi, u, wt, lat, near, far, *halos)


def spread(var_at, x, parts):
    ch, cells = parts[0].shape
    lat = 64
    place = lax.broadcasted_iota(jnp.int32, (1, cells), 1) % lat
    for d, v in enumerate(parts):
        rs = pl.ds(pl.multiple_of(((var_at - d) & 3) * ch, ch), ch)
        zero = jnp.zeros_like(v)
        up = jnp.where(place == 0, zero, pltpu.roll(v, 1, 1))
        down = jnp.where(place == lat - 1, zero, pltpu.roll(v, cells - 1, 1))
        for r, u in enumerate((up, v, down)):
            x[r, rs, :] = u
            x[3 + r, rs, :] = pltpu.roll(u, cells - lat, 1)


def hidden_taps(x, weights):
    bf = x.dtype
    lat = 64
    width = x.shape[2] - 2 * lat
    last = jnp.concatenate([w[9] for w in weights], axis=0).astype(jnp.float32)
    mix = last.T[:216].astype(bf)
    bias = last[:, 216:217] + last[:, 217:218] + last[:, 218:219]
    kernel_w = jnp.concatenate(
        [jnp.concatenate([w[k] for w in weights], axis=0) for k in range(9)], axis=1)
    cols = []
    for r in range(3):
        for s in range(3):
            src, off = (3 + r, 0) if s == 1 else (r, s * lat)
            cols.append(x[src, :, off:off + width])
    pre = jnp.dot(kernel_w, jnp.concatenate(cols, axis=0), preferred_element_type=jnp.float32) + bias
    hidden = pre * (0.5 * jnp.tanh(0.5 * pre) + 0.5)
    return jnp.dot(mix, hidden.astype(bf), preferred_element_type=jnp.float32)


def inner_kernel(var_ref, inner_ref, *rest):
    weights = rest[:8]
    taps_ref, x = rest[8:]
    spread(var_ref[0], x, [inner_ref[(var_ref[0] - d) & 3] for d in range(4)])
    taps_ref[...] = hidden_taps(x, weights)


def outer_kernel(var_ref, inner_taps_ref, inner_ref, *rest):
    outer, weights = rest[:4], rest[4:12]
    out_ref, x, taps, rows, pairs = rest[12:]
    lat = 64
    cells = inner_ref.shape[2]
    inner = [inner_ref[(var_ref[0] - d) & 3] for d in range(4)]
    hid_cells = 2 * cells - 2 * lat
    out_cells = hid_cells - 2 * lat

    spread(var_ref[0], x, [
        jnp.concatenate([o[:, :128], i[:, :128], i[:, cells - 128:], o[:, 128:]], axis=1)
        for i, o in zip(inner, outer)])
    mine = hidden_taps(x, weights)
    taps[:, :128] = mine[:, :128]
    taps[:, 128:cells] = inner_taps_ref[...]
    taps[:, cells:] = mine[:, 256:]

    def total(r):
        y = [taps[(3 * r + s) * 24:(3 * r + s + 1) * 24, :] for s in range(3)]
        mid = pltpu.roll(y[1], hid_cells - lat, 1)
        return y[0][:, :out_cells] + mid[:, :out_cells] + y[2][:, 2 * lat:2 * lat + out_cells]

    spot = lax.broadcasted_iota(jnp.int32, (1, out_cells), 1) % lat
    full = jnp.where(spot == 0, 0.0, pltpu.roll(total(0), 1, 1))
    full = full + total(1)
    full = full + jnp.where(spot == lat - 1, 0.0, pltpu.roll(total(2), out_cells - 1, 1))
    shift = []
    for g in range(4):
        at = (var_ref[0] - g) & 3
        terms = jnp.zeros((16, 256), jnp.float32)
        for d in range(4):
            terms = jnp.where(at == d, weights[d][9, 0:16, :].astype(jnp.float32), terms)
        shift.append((terms[:, 219:220] + terms[:, 220:221] + terms[:, 221:222])[:6])
    full = full + jnp.concatenate(shift, axis=0)

    rows[...] = jnp.zeros_like(rows)
    for l in range(32):
        col = full[:, l * lat:(l + 1) * lat]
        for g in range(4):
            rows[pl.ds(g * 256 + l, 6, stride=32), :] = col[g * 6:g * 6 + 6]
    turned = rows[...].T
    for g in range(4):
        for h in range(2):
            pairs[pl.ds(g * 2 * lat + h, lat, stride=2), :] = turned[:, g * 256 + h * 128:g * 256 + h * 128 + 128]
    out_ref[...] = pairs[...].astype(out_ref.dtype)


def convolve_inner(var_at, inner, weights):
    _, ch, cells = inner.shape
    smem = pl.BlockSpec(memory_space=pltpu.SMEM)
    vmem = pl.BlockSpec(memory_space=pltpu.VMEM)
    return pl.pallas_call(
        inner_kernel,
        out_shape=jax.ShapeDtypeStruct((216, cells - 128), jnp.float32),
        in_specs=[smem] + [vmem] * 9,
        out_specs=vmem,
        scratch_shapes=[pltpu.VMEM((6, 4 * ch, cells), inner.dtype)],
        cost_estimate=pl.CostEstimate(flops=2 * 512 * 2304 * cells, bytes_accessed=1 << 22, transcendentals=512 * cells),
        compiler_params=pltpu.CompilerParams(vmem_limit_bytes=LIMIT << 20),
    )(var_at, inner, *weights)


def convolve_outer(var_at, inner_taps, inner, outer, weights):
    _, ch, cells = inner.shape
    smem = pl.BlockSpec(memory_space=pltpu.SMEM)
    vmem = pl.BlockSpec(memory_space=pltpu.VMEM)
    return pl.pallas_call(
        outer_kernel,
        out_shape=jax.ShapeDtypeStruct((512, 128), inner.dtype),
        in_specs=[smem] + [vmem] * 14,
        out_specs=vmem,
        scratch_shapes=[
            pltpu.VMEM((6, 4 * ch, cells + 256), inner.dtype),
            pltpu.VMEM((216, 2 * cells - 128), jnp.float32),
            pltpu.VMEM((1024, 64), jnp.float32),
            pltpu.VMEM((512, 128), jnp.float32),
        ],
        cost_estimate=pl.CostEstimate(flops=2 * 512 * 2304 * cells, bytes_accessed=1 << 22, transcendentals=512 * cells),
        compiler_params=pltpu.CompilerParams(vmem_limit_bytes=LIMIT << 20),
    )(var_at, inner_taps, inner, *outer, *weights)


def finish_kernel(got_ref, out_ref, pairs):
    pairs[...] = got_ref[...].astype(jnp.float32)
    for k in range(6):
        half, lane = k // 4, k % 4 * 32
        out_ref[k] = jnp.concatenate(
            [pairs[pl.ds(128 * v + half, 64, stride=2), :][:, lane:lane + 32] for v in range(4)], axis=1)


def finish(got):
    vmem = pl.BlockSpec(memory_space=pltpu.VMEM)
    return pl.pallas_call(
        finish_kernel,
        out_shape=jax.ShapeDtypeStruct((6, 64, 128), jnp.float32),
        in_specs=[vmem],
        out_specs=vmem,
        scratch_shapes=[pltpu.VMEM((512, 128), jnp.float32)],
    )(got)


def pack_kernel(core_ref, bias2_ref, first_ref, second_ref, bias1_ref, out_ref):
    half = first_ref.shape[1] // 2
    bf = out_ref.dtype
    at = core_ref[0]
    out_ref[:9] = first_ref[:, pl.ds(pl.multiple_of(at * half, half), half), :]
    lane = lax.broadcasted_iota(jnp.int32, (1, 2 * half), 1) % half
    bias2 = jnp.zeros((1, 2 * half), jnp.float32)
    for k in range(bias2_ref.shape[0]):
        bias2 = jnp.where(lane == k, bias2_ref[k], bias2)
    terms = []
    for value in (bias1_ref[...], bias2):
        for _ in range(3):
            term = value.astype(bf).astype(jnp.float32)
            value = value - term
            terms.append(term)
    second = [second_ref[k].astype(jnp.float32) for k in range(9)]
    columns = jnp.concatenate(second + terms + [jnp.zeros((34, 2 * half), jnp.float32)], axis=0).T
    out_ref[9] = jnp.where(at == 0, columns[:half], columns[half:]).astype(bf)


def over_var(parts):
    count = lax.axis_size("var")
    return [parts[0]] + [
        lax.ppermute(parts[d], "var", [(i, (i + d) % count) for i in range(count)]) for d in range(1, count)]


def gathered_weights(conv1_weight, conv1_bias, conv2_weight, conv2_bias):
    smem = pl.BlockSpec(memory_space=pltpu.SMEM)
    vmem = pl.BlockSpec(memory_space=pltpu.VMEM)
    taps, channels, inputs = conv1_weight.shape
    mine = pl.pallas_call(
        pack_kernel,
        out_shape=jax.ShapeDtypeStruct((taps + 1, channels // 2, inputs), conv1_weight.dtype),
        in_specs=[smem] * 2 + [vmem] * 3,
        out_specs=vmem,
    )((lax.axis_index("tile") % 2).reshape(1), conv2_bias, conv1_weight, conv2_weight, conv1_bias.reshape(1, channels))
    return over_var([mine] * 4)


def exchanged_weights(blocks):
    tiles = lax.axis_size("tile")
    return blocks + [lax.ppermute(b, "tile", [(i, i ^ 1) for i in range(tiles)]) for b in blocks]


def body(mesh_latents, edge_idx, edge_weight, conv1_weight, conv1_bias, conv2_weight, conv2_bias):
    tile_at = lax.axis_index("tile")
    tiles = lax.axis_size("tile")
    mesh_dev = mesh_latents.shape[1]
    rim = 64
    core = tile_at % 2
    near = [(i, i ^ 1) for i in range(tiles)]
    far = [(i, (i + 1 if i % 2 else i - 1) % tiles) for i in range(tiles)]
    head, tail = mesh_latents[:, :rim], mesh_latents[:, mesh_dev - rim:]
    near_halo = lax.ppermute(jnp.where(core == 0, tail, head), "tile", near)
    far_halo = lax.ppermute(jnp.where(core == 0, head, tail), "tile", far)
    blocks = gathered_weights(conv1_weight, conv1_bias, conv2_weight, conv2_bias)
    u, wt, lo, hi = prep(edge_idx, edge_weight, tile_at, mesh_dev, mesh_dev * tiles, rim)
    var_at = lax.axis_index("var").reshape(1)
    at = jnp.concatenate([var_at, core.reshape(1)])
    nodes = (at, u, wt, lo, hi, mesh_latents, near_halo, far_halo)
    to_near, to_far = decode("edges", *nodes)
    near_out = lax.ppermute(to_near, "tile", near)
    far_out = lax.ppermute(to_far, "tile", far)
    nodes, _, _ = lax.optimization_barrier((nodes, to_near, to_far))
    inner, = decode("inner", *nodes)
    inner, near_out, far_out = lax.optimization_barrier((inner, near_out, far_out))
    inner = lax.all_to_all(inner, "var", split_axis=0, concat_axis=0, tiled=True)
    outer = decode("outer", *nodes, near_out, far_out)
    outer, blocks = lax.optimization_barrier((outer, blocks))
    weights = exchanged_weights(blocks)
    outer = over_var(outer)
    inner_taps = convolve_inner(var_at, inner, weights)
    fields = convolve_outer(var_at, inner_taps, inner, outer, weights)
    got = lax.all_to_all(fields.reshape(256, 2, 128), ("var", "tile"), split_axis=0, concat_axis=0, tiled=True)
    return finish(got.reshape(512, 128)).reshape(6, 1, tiles * 128)


def solution(mesh):
    return jax.shard_map(
        body,
        mesh=mesh,
        in_specs=(
            P("var", "tile"),
            P(None, None, "tile"),
            P(None, None, "tile"),
            P(None, "var", None),
            P("var"),
            P(None, None, "var"),
            P("var"),
        ),
        out_specs=P("var", "tile", None),
        check_vma=False,
    )
```

```python
import functools

import jax
import jax.numpy as jnp
from jax import lax
from jax.experimental import pallas as pl
from jax.experimental.pallas import tpu as pltpu
from jax.sharding import PartitionSpec as P


def prep(edge_idx, edge_weight, tile_at, mesh_dev, nmesh, rim):
    u = jnp.mod(edge_idx - tile_at * mesh_dev + rim, nmesh)
    u = u.transpose(0, 2, 1).reshape(3, -1, 128)
    wt = edge_weight.transpose(0, 2, 1).reshape(3, -1, 128)
    lo = jnp.min(u, axis=(0, 2)) // 64
    hi = jnp.max(u, axis=(0, 2)) // 64
    return u, wt, lo, hi

LIMIT = 16
INNER = 10


def decode_kernel(part, at_ref, lo_ref, hi_ref, u_ref, wt_ref, lat_ref, near_ref, far_ref, *rest):
    even = at_ref[1] == 0
    sides = lambda near, far: (jnp.where(even, far, near), jnp.where(even, near, far))
    left, right = sides(near_ref[...], far_ref[...])
    if part in ("outer", "own"):
        near_out_ref, far_out_ref, *rest = rest
        before, after = sides(near_out_ref[...], far_out_ref[...])
    outs, (lats, parts, accs) = rest[:-3], rest[-3:]
    ch, nodes = lat_ref.shape
    rim = near_ref.shape[1]
    ext = nodes + 2 * rim
    nblk = u_ref.shape[1]
    width = lats.shape[2]
    bf = lat_ref.dtype
    main = lat_ref[...]
    zeros = lambda n: jnp.zeros((ch, n), bf)
    lats[0] = jnp.concatenate([left, main, right, zeros(width - ext)], axis=1)
    lats[1] = jnp.concatenate([main, right, zeros(width - ext + rim)], axis=1)

    u0, u1, u2 = u_ref[0], u_ref[1], u_ref[2]
    w0, w1, w2 = wt_ref[0], wt_ref[1], wt_ref[2]
    w0 = w0 + jnp.where(u1 == u0, w1, 0.0) + jnp.where(u2 == u0, w2, 0.0)
    w1 = w1 + jnp.where(u2 == u1, w2, 0.0)
    for k, w in enumerate((w0, w1, w2)):
        top = w.astype(bf).astype(jnp.float32)
        parts[k] = top
        parts[3 + k] = w - top

    node = lax.broadcasted_iota(jnp.int32, (256, 128), 0).astype(jnp.float32).astype(bf)

    def window(b, at):
        src = lats[at & 1, :, pl.ds(pl.multiple_of((at >> 1) * 128, 128), 256)]
        tops = jnp.zeros((256, 128), bf)
        rests = jnp.zeros((256, 128), bf)
        for k in (2, 1, 0):
            rel = (u_ref[k, pl.ds(b, 1), :] - at * 64).astype(jnp.float32).astype(bf)
            here = node == rel
            tops = jnp.where(here, parts[k, pl.ds(b, 1), :].astype(bf), tops)
            rests = jnp.where(here, parts[3 + k, pl.ds(b, 1), :].astype(bf), rests)
        table = jnp.concatenate([tops, rests], axis=1)
        both = jnp.dot(src, table, preferred_element_type=jnp.float32)
        return both[:, :128] + both[:, 128:]

    def several(ids):
        more = jnp.int32(0)
        for j, b in enumerate(ids):
            at = lo_ref[b]
            accs[j] = window(b, at)
            more = more + jnp.where(hi_ref[b] - at >= 4, 1, 0)

        @pl.when(more > 0)
        def _():
            for j, b in enumerate(ids):
                at = lo_ref[b]

                @pl.loop(1, ((hi_ref[b] - at) >> 2) + 1)
                def _(step):
                    accs[j] += window(b, at + 4 * step)

    if part == "edges":
        several((0, nblk - 1))
        first, last = accs[0].astype(bf), accs[1].astype(bf)
        outs[0][...] = jnp.where(even, last, first)
        outs[1][...] = jnp.where(even, first, last)
        return

    per = nblk // 4
    outer = per + 1 - INNER
    for d in {"inner": range(4), "outer": range(1, 4), "own": range(1)}[part]:
        v = (at_ref[0] + d) & 3
        if part == "inner":
            several([v * per + j for j in range(INNER)])
            for j in range(INNER):
                outs[0][v, :, j * 128:j * 128 + 128] = accs[j].astype(bf)
            continue
        out = outs[max(d - 1, 0)]
        several([jnp.maximum(v * per - 1, 0)] + [jnp.minimum(v * per + INNER + j, nblk - 1) for j in range(outer)])
        out[:, :128] = jnp.where(v == 0, before, accs[0].astype(bf))
        for j in range(1, outer):
            out[:, j * 128:j * 128 + 128] = accs[j].astype(bf)
        out[:, outer * 128:] = jnp.where(v == 3, after, accs[outer].astype(bf))


def decode(part, at, u, wt, lo, hi, lat, near, far, *halos):
    ch, nodes = lat.shape
    nblk = u.shape[1]
    smem = pl.BlockSpec(memory_space=pltpu.SMEM)
    vmem = pl.BlockSpec(memory_space=pltpu.VMEM)
    group = INNER
    if part == "edges":
        shapes, done = (jax.ShapeDtypeStruct((ch, 128), lat.dtype),) * 2, 2
    elif part == "inner":
        shapes, done = (jax.ShapeDtypeStruct((4, ch, group * 128), lat.dtype),), nblk // 2
    else:
        count = 3 if part == "outer" else 1
        shapes, done = (jax.ShapeDtypeStruct((ch, (nblk // 4 + 2 - group) * 128), lat.dtype),) * count, 8 * count
    return pl.pallas_call(
        functools.partial(decode_kernel, part),
        out_shape=shapes,
        in_specs=[smem] * 3 + [vmem] * (5 + len(halos)),
        out_specs=(vmem,) * len(shapes),
        scratch_shapes=[
            pltpu.VMEM((2, ch, nodes + 384), lat.dtype),
            pltpu.VMEM((6, nblk, 128), jnp.float32),
            pltpu.VMEM((group, ch, 128), jnp.float32),
        ],
        cost_estimate=pl.CostEstimate(flops=done * 256 * 128 * 4 * ch * 16, bytes_accessed=2 * ch * nodes * 2, transcendentals=0),
        compiler_params=pltpu.CompilerParams(vmem_limit_bytes=8 << 20),
    )(at, lo, hi, u, wt, lat, near, far, *halos)


def spread(var_at, x, parts):
    ch, cells = parts[0].shape
    lat = 64
    place = lax.broadcasted_iota(jnp.int32, (1, cells), 1) % lat
    for d, v in enumerate(parts):
        rs = pl.ds(pl.multiple_of(((var_at - d) & 3) * ch, ch), ch)
        zero = jnp.zeros_like(v)
        up = jnp.where(place == 0, zero, pltpu.roll(v, 1, 1))
        down = jnp.where(place == lat - 1, zero, pltpu.roll(v, cells - 1, 1))
        for r, u in enumerate((up, v, down)):
            x[r, rs, :] = u
            x[3 + r, rs, :] = pltpu.roll(u, cells - lat, 1)


def hidden_taps(x, weights):
    bf = x.dtype
    lat = 64
    width = x.shape[2] - 2 * lat
    last = jnp.concatenate([w[9] for w in weights], axis=0).astype(jnp.float32)
    mix = last.T[:216].astype(bf)
    bias = last[:, 216:217] + last[:, 217:218] + last[:, 218:219]
    kernel_w = jnp.concatenate(
        [jnp.concatenate([w[k] for w in weights], axis=0) for k in range(9)], axis=1)
    cols = []
    for r in range(3):
        for s in range(3):
            src, off = (3 + r, 0) if s == 1 else (r, s * lat)
            cols.append(x[src, :, off:off + width])
    pre = jnp.dot(kernel_w, jnp.concatenate(cols, axis=0), preferred_element_type=jnp.float32) + bias
    hidden = pre * (0.5 * jnp.tanh(0.5 * pre) + 0.5)
    return jnp.dot(mix, hidden.astype(bf), preferred_element_type=jnp.float32)


def inner_kernel(var_ref, inner_ref, *rest):
    weights = rest[:8]
    taps_ref, x = rest[8:]
    spread(var_ref[0], x, [inner_ref[(var_ref[0] - d) & 3] for d in range(4)])
    taps_ref[...] = hidden_taps(x, weights)


def outer_kernel(var_ref, inner_taps_ref, inner_ref, *rest):
    outer, weights = rest[:4], rest[4:12]
    out_ref, x, taps, rows, pairs = rest[12:]
    lat = 64
    cells = inner_ref.shape[2]
    hid_cells = cells + outer[0].shape[1] - 2 * lat
    inner = [inner_ref[(var_ref[0] - d) & 3] for d in range(4)]
    out_cells = hid_cells - 2 * lat

    spread(var_ref[0], x, [
        jnp.concatenate([o[:, :128], i[:, :128], i[:, cells - 128:], o[:, 128:]], axis=1)
        for i, o in zip(inner, outer)])
    mine = hidden_taps(x, weights)
    taps[:, :128] = mine[:, :128]
    taps[:, 128:cells] = inner_taps_ref[...]
    taps[:, cells:] = mine[:, 256:]

    def total(r):
        y = [taps[(3 * r + s) * 24:(3 * r + s + 1) * 24, :] for s in range(3)]
        mid = pltpu.roll(y[1], hid_cells - lat, 1)
        return y[0][:, :out_cells] + mid[:, :out_cells] + y[2][:, 2 * lat:2 * lat + out_cells]

    spot = lax.broadcasted_iota(jnp.int32, (1, out_cells), 1) % lat
    full = jnp.where(spot == 0, 0.0, pltpu.roll(total(0), 1, 1))
    full = full + total(1)
    full = full + jnp.where(spot == lat - 1, 0.0, pltpu.roll(total(2), out_cells - 1, 1))
    shift = []
    for g in range(4):
        at = (var_ref[0] - g) & 3
        terms = jnp.zeros((16, 256), jnp.float32)
        for d in range(4):
            terms = jnp.where(at == d, weights[d][9, 0:16, :].astype(jnp.float32), terms)
        shift.append((terms[:, 219:220] + terms[:, 220:221] + terms[:, 221:222])[:6])
    full = full + jnp.concatenate(shift, axis=0)

    rows[...] = jnp.zeros_like(rows)
    for l in range(32):
        col = full[:, l * lat:(l + 1) * lat]
        for g in range(4):
            rows[pl.ds(g * 256 + l, 6, stride=32), :] = col[g * 6:g * 6 + 6]
    turned = rows[...].T
    for g in range(4):
        for h in range(2):
            pairs[pl.ds(g * 2 * lat + h, lat, stride=2), :] = turned[:, g * 256 + h * 128:g * 256 + h * 128 + 128]
    out_ref[...] = pairs[...].astype(out_ref.dtype)


def convolve_inner(var_at, inner, weights):
    _, ch, cells = inner.shape
    smem = pl.BlockSpec(memory_space=pltpu.SMEM)
    vmem = pl.BlockSpec(memory_space=pltpu.VMEM)
    return pl.pallas_call(
        inner_kernel,
        out_shape=jax.ShapeDtypeStruct((216, cells - 128), jnp.float32),
        in_specs=[smem] + [vmem] * 9,
        out_specs=vmem,
        scratch_shapes=[pltpu.VMEM((6, 4 * ch, cells), inner.dtype)],
        cost_estimate=pl.CostEstimate(flops=2 * 512 * 2304 * cells, bytes_accessed=1 << 22, transcendentals=512 * cells),
        compiler_params=pltpu.CompilerParams(vmem_limit_bytes=LIMIT << 20),
    )(var_at, inner, *weights)


def convolve_outer(var_at, inner_taps, inner, outer, weights):
    _, ch, cells = inner.shape
    rest = outer[0].shape[1]
    smem = pl.BlockSpec(memory_space=pltpu.SMEM)
    vmem = pl.BlockSpec(memory_space=pltpu.VMEM)
    return pl.pallas_call(
        outer_kernel,
        out_shape=jax.ShapeDtypeStruct((512, 128), inner.dtype),
        in_specs=[smem] + [vmem] * 14,
        out_specs=vmem,
        scratch_shapes=[
            pltpu.VMEM((6, 4 * ch, rest + 256), inner.dtype),
            pltpu.VMEM((216, cells + rest - 128), jnp.float32),
            pltpu.VMEM((1024, 64), jnp.float32),
            pltpu.VMEM((512, 128), jnp.float32),
        ],
        cost_estimate=pl.CostEstimate(flops=2 * 512 * 2304 * cells, bytes_accessed=1 << 22, transcendentals=512 * cells),
        compiler_params=pltpu.CompilerParams(vmem_limit_bytes=LIMIT << 20),
    )(var_at, inner_taps, inner, *outer, *weights)


def finish_kernel(got_ref, out_ref, pairs):
    pairs[...] = got_ref[...].astype(jnp.float32)
    for k in range(6):
        half, lane = k // 4, k % 4 * 32
        out_ref[k] = jnp.concatenate(
            [pairs[pl.ds(128 * v + half, 64, stride=2), :][:, lane:lane + 32] for v in range(4)], axis=1)


def finish(got):
    vmem = pl.BlockSpec(memory_space=pltpu.VMEM)
    return pl.pallas_call(
        finish_kernel,
        out_shape=jax.ShapeDtypeStruct((6, 64, 128), jnp.float32),
        in_specs=[vmem],
        out_specs=vmem,
        scratch_shapes=[pltpu.VMEM((512, 128), jnp.float32)],
    )(got)


def pack_kernel(core_ref, bias2_ref, first_ref, second_ref, bias1_ref, out_ref):
    half = first_ref.shape[1] // 2
    bf = out_ref.dtype
    at = core_ref[0]
    out_ref[:9] = first_ref[:, pl.ds(pl.multiple_of(at * half, half), half), :]
    lane = lax.broadcasted_iota(jnp.int32, (1, 2 * half), 1) % half
    bias2 = jnp.zeros((1, 2 * half), jnp.float32)
    for k in range(bias2_ref.shape[0]):
        bias2 = jnp.where(lane == k, bias2_ref[k], bias2)
    terms = []
    for value in (bias1_ref[...], bias2):
        for _ in range(3):
            term = value.astype(bf).astype(jnp.float32)
            value = value - term
            terms.append(term)
    second = [second_ref[k].astype(jnp.float32) for k in range(9)]
    columns = jnp.concatenate(second + terms + [jnp.zeros((34, 2 * half), jnp.float32)], axis=0).T
    out_ref[9] = jnp.where(at == 0, columns[:half], columns[half:]).astype(bf)


def over_var(parts):
    count = lax.axis_size("var")
    return [parts[0]] + [
        lax.ppermute(parts[d], "var", [(i, (i + d) % count) for i in range(count)]) for d in range(1, count)]


def gathered_weights(conv1_weight, conv1_bias, conv2_weight, conv2_bias):
    smem = pl.BlockSpec(memory_space=pltpu.SMEM)
    vmem = pl.BlockSpec(memory_space=pltpu.VMEM)
    taps, channels, inputs = conv1_weight.shape
    mine = pl.pallas_call(
        pack_kernel,
        out_shape=jax.ShapeDtypeStruct((taps + 1, channels // 2, inputs), conv1_weight.dtype),
        in_specs=[smem] * 2 + [vmem] * 3,
        out_specs=vmem,
    )((lax.axis_index("tile") % 2).reshape(1), conv2_bias, conv1_weight, conv2_weight, conv1_bias.reshape(1, channels))
    return over_var([mine] * 4)


def exchanged_weights(blocks):
    tiles = lax.axis_size("tile")
    return blocks + [lax.ppermute(b, "tile", [(i, i ^ 1) for i in range(tiles)]) for b in blocks]


def body(mesh_latents, edge_idx, edge_weight, conv1_weight, conv1_bias, conv2_weight, conv2_bias):
    tile_at = lax.axis_index("tile")
    tiles = lax.axis_size("tile")
    mesh_dev = mesh_latents.shape[1]
    rim = 64
    core = tile_at % 2
    near = [(i, i ^ 1) for i in range(tiles)]
    far = [(i, (i + 1 if i % 2 else i - 1) % tiles) for i in range(tiles)]
    head, tail = mesh_latents[:, :rim], mesh_latents[:, mesh_dev - rim:]
    near_halo = lax.ppermute(jnp.where(core == 0, tail, head), "tile", near)
    far_halo = lax.ppermute(jnp.where(core == 0, head, tail), "tile", far)
    blocks = gathered_weights(conv1_weight, conv1_bias, conv2_weight, conv2_bias)
    u, wt, lo, hi = prep(edge_idx, edge_weight, tile_at, mesh_dev, mesh_dev * tiles, rim)
    var_at = lax.axis_index("var").reshape(1)
    at = jnp.concatenate([var_at, core.reshape(1)])
    nodes = (at, u, wt, lo, hi, mesh_latents, near_halo, far_halo)
    to_near, to_far = decode("edges", *nodes)
    near_out = lax.ppermute(to_near, "tile", near)
    far_out = lax.ppermute(to_far, "tile", far)
    nodes, _, _ = lax.optimization_barrier((nodes, to_near, to_far))
    inner, = decode("inner", *nodes)
    inner, near_out, far_out = lax.optimization_barrier((inner, near_out, far_out))
    inner = lax.all_to_all(inner, "var", split_axis=0, concat_axis=0, tiled=True)
    outer = decode("outer", *nodes, near_out, far_out)
    outer, blocks = lax.optimization_barrier((outer, blocks))
    weights = exchanged_weights(blocks)
    outer = over_var([None] + list(outer))
    inner_taps = convolve_inner(var_at, inner, weights)
    nodes, near_out, far_out, inner_taps = lax.optimization_barrier((nodes, near_out, far_out, inner_taps))
    outer[0], = decode("own", *nodes, near_out, far_out)
    fields = convolve_outer(var_at, inner_taps, inner, outer, weights)
    got = lax.all_to_all(fields.reshape(256, 2, 128), ("var", "tile"), split_axis=0, concat_axis=0, tiled=True)
    return finish(got.reshape(512, 128)).reshape(6, 1, tiles * 128)


def solution(mesh):
    return jax.shard_map(
        body,
        mesh=mesh,
        in_specs=(
            P("var", "tile"),
            P(None, None, "tile"),
            P(None, None, "tile"),
            P(None, "var", None),
            P("var"),
            P(None, None, "var"),
            P("var"),
        ),
        out_specs=P("var", "tile", None),
        check_vma=False,
    )
```

```python
import functools

import jax
import jax.numpy as jnp
from jax import lax
from jax.experimental import pallas as pl
from jax.experimental.pallas import tpu as pltpu
from jax.sharding import PartitionSpec as P


def prep(edge_idx, edge_weight, tile_at, mesh_dev, nmesh, rim):
    u = jnp.mod(edge_idx - tile_at * mesh_dev + rim, nmesh)
    u = u.transpose(0, 2, 1).reshape(3, -1, 128)
    wt = edge_weight.transpose(0, 2, 1).reshape(3, -1, 128)
    lo = jnp.min(u, axis=(0, 2)) // 64
    hi = jnp.max(u, axis=(0, 2)) // 64
    return u, wt, lo, hi

LIMIT = 16
INNER = 10


def decode_kernel(part, at_ref, lo_ref, hi_ref, u_ref, wt_ref, lat_ref, near_ref, far_ref, *rest):
    even = at_ref[1] == 0
    sides = lambda near, far: (jnp.where(even, far, near), jnp.where(even, near, far))
    left, right = sides(near_ref[...], far_ref[...])
    if part in ("outer", "own"):
        near_out_ref, far_out_ref, *rest = rest
        before, after = sides(near_out_ref[...], far_out_ref[...])
    outs, (lats, parts, accs) = rest[:-3], rest[-3:]
    ch, nodes = lat_ref.shape
    rim = near_ref.shape[1]
    ext = nodes + 2 * rim
    nblk = u_ref.shape[1]
    width = lats.shape[2]
    bf = lat_ref.dtype
    main = lat_ref[...]
    zeros = lambda n: jnp.zeros((ch, n), bf)
    lats[0] = jnp.concatenate([left, main, right, zeros(width - ext)], axis=1)
    lats[1] = jnp.concatenate([main, right, zeros(width - ext + rim)], axis=1)

    u0, u1, u2 = u_ref[0], u_ref[1], u_ref[2]
    w0, w1, w2 = wt_ref[0], wt_ref[1], wt_ref[2]
    w0 = w0 + jnp.where(u1 == u0, w1, 0.0) + jnp.where(u2 == u0, w2, 0.0)
    w1 = w1 + jnp.where(u2 == u1, w2, 0.0)
    for k, w in enumerate((w0, w1, w2)):
        top = w.astype(bf).astype(jnp.float32)
        parts[k] = top
        parts[3 + k] = w - top

    node = lax.broadcasted_iota(jnp.int32, (256, 128), 0).astype(jnp.float32).astype(bf)

    def window(b, at):
        src = lats[at & 1, :, pl.ds(pl.multiple_of((at >> 1) * 128, 128), 256)]
        tops = jnp.zeros((256, 128), bf)
        rests = jnp.zeros((256, 128), bf)
        for k in (2, 1, 0):
            rel = (u_ref[k, pl.ds(b, 1), :] - at * 64).astype(jnp.float32).astype(bf)
            here = node == rel
            tops = jnp.where(here, parts[k, pl.ds(b, 1), :].astype(bf), tops)
            rests = jnp.where(here, parts[3 + k, pl.ds(b, 1), :].astype(bf), rests)
        table = jnp.concatenate([tops, rests], axis=1)
        both = jnp.dot(src, table, preferred_element_type=jnp.float32)
        return both[:, :128] + both[:, 128:]

    def several(ids):
        more = jnp.int32(0)
        for j, b in enumerate(ids):
            at = lo_ref[b]
            accs[j] = window(b, at)
            more = more + jnp.where(hi_ref[b] - at >= 4, 1, 0)

        @pl.when(more > 0)
        def _():
            for j, b in enumerate(ids):
                at = lo_ref[b]

                @pl.loop(1, ((hi_ref[b] - at) >> 2) + 1)
                def _(step):
                    accs[j] += window(b, at + 4 * step)

    if part == "edges":
        several((0, nblk - 1))
        first, last = accs[0].astype(bf), accs[1].astype(bf)
        outs[0][...] = jnp.where(even, last, first)
        outs[1][...] = jnp.where(even, first, last)
        return

    per = nblk // 4
    outer = per + 1 - INNER
    for d in {"inner": range(4), "outer": range(1, 4), "own": range(1)}[part]:
        v = (at_ref[0] + d) & 3
        if part == "inner":
            several([v * per + j for j in range(INNER)])
            for j in range(INNER):
                outs[0][v, :, j * 128:j * 128 + 128] = accs[j].astype(bf)
            continue
        out = outs[max(d - 1, 0)]
        several([jnp.maximum(v * per - 1, 0)] + [jnp.minimum(v * per + INNER + j, nblk - 1) for j in range(outer)])
        out[:, :128] = jnp.where(v == 0, before, accs[0].astype(bf))
        for j in range(1, outer):
            out[:, j * 128:j * 128 + 128] = accs[j].astype(bf)
        out[:, outer * 128:] = jnp.where(v == 3, after, accs[outer].astype(bf))


def decode(part, at, u, wt, lo, hi, lat, near, far, *halos):
    ch, nodes = lat.shape
    nblk = u.shape[1]
    smem = pl.BlockSpec(memory_space=pltpu.SMEM)
    vmem = pl.BlockSpec(memory_space=pltpu.VMEM)
    group = INNER
    if part == "edges":
        shapes, done = (jax.ShapeDtypeStruct((ch, 128), lat.dtype),) * 2, 2
    elif part == "inner":
        shapes, done = (jax.ShapeDtypeStruct((4, ch, group * 128), lat.dtype),), nblk // 2
    else:
        count = 3 if part == "outer" else 1
        shapes, done = (jax.ShapeDtypeStruct((ch, (nblk // 4 + 2 - group) * 128), lat.dtype),) * count, 8 * count
    return pl.pallas_call(
        functools.partial(decode_kernel, part),
        out_shape=shapes,
        in_specs=[smem] * 3 + [vmem] * (5 + len(halos)),
        out_specs=(vmem,) * len(shapes),
        scratch_shapes=[
            pltpu.VMEM((2, ch, nodes + 384), lat.dtype),
            pltpu.VMEM((6, nblk, 128), jnp.float32),
            pltpu.VMEM((group, ch, 128), jnp.float32),
        ],
        cost_estimate=pl.CostEstimate(flops=done * 256 * 128 * 4 * ch * 16, bytes_accessed=2 * ch * nodes * 2, transcendentals=0),
        compiler_params=pltpu.CompilerParams(vmem_limit_bytes=8 << 20),
    )(at, lo, hi, u, wt, lat, near, far, *halos)


def spread(var_at, x, parts):
    ch, cells = parts[0].shape
    lat = 64
    place = lax.broadcasted_iota(jnp.int32, (1, cells), 1) % lat
    for d, v in enumerate(parts):
        rs = pl.ds(pl.multiple_of(((var_at - d) & 3) * ch, ch), ch)
        zero = jnp.zeros_like(v)
        up = jnp.where(place == 0, zero, pltpu.roll(v, 1, 1))
        down = jnp.where(place == lat - 1, zero, pltpu.roll(v, cells - 1, 1))
        for r, u in enumerate((up, v, down)):
            x[r, rs, :] = u
            x[3 + r, rs, :] = pltpu.roll(u, cells - lat, 1)


def hidden_taps(x, weights):
    bf = x.dtype
    lat = 64
    width = x.shape[2] - 2 * lat
    last = jnp.concatenate([w[9] for w in weights], axis=0).astype(jnp.float32)
    mix = last.T[:216].astype(bf)
    bias = last[:, 216:217] + last[:, 217:218] + last[:, 218:219]
    kernel_w = jnp.concatenate(
        [jnp.concatenate([w[k] for w in weights], axis=0) for k in range(9)], axis=1)
    cols = []
    for r in range(3):
        for s in range(3):
            src, off = (3 + r, 0) if s == 1 else (r, s * lat)
            cols.append(x[src, :, off:off + width])
    pre = jnp.dot(kernel_w, jnp.concatenate(cols, axis=0), preferred_element_type=jnp.float32) + bias
    hidden = pre * (0.5 * jnp.tanh(0.5 * pre) + 0.5)
    return jnp.dot(mix, hidden.astype(bf), preferred_element_type=jnp.float32)


def inner_kernel(var_ref, inner_ref, *rest):
    weights = rest[:8]
    taps_ref, x = rest[8:]
    spread(var_ref[0], x, [inner_ref[(var_ref[0] - d) & 3] for d in range(4)])
    taps_ref[...] = hidden_taps(x, weights)


def outer_kernel(var_ref, inner_taps_ref, inner_ref, *rest):
    outer, weights = rest[:4], rest[4:12]
    out_ref, x, taps, rows, pairs = rest[12:]
    lat = 64
    cells = inner_ref.shape[2]
    hid_cells = cells + outer[0].shape[1] - 2 * lat
    inner = [inner_ref[(var_ref[0] - d) & 3] for d in range(4)]
    out_cells = hid_cells - 2 * lat

    spread(var_ref[0], x, [
        jnp.concatenate([o[:, :128], i[:, :128], i[:, cells - 128:], o[:, 128:]], axis=1)
        for i, o in zip(inner, outer)])
    mine = hidden_taps(x, weights)
    taps[:, :128] = mine[:, :128]
    taps[:, 128:cells] = inner_taps_ref[...]
    taps[:, cells:] = mine[:, 256:]

    def total(r):
        y = [taps[(3 * r + s) * 24:(3 * r + s + 1) * 24, :] for s in range(3)]
        mid = pltpu.roll(y[1], hid_cells - lat, 1)
        return y[0][:, :out_cells] + mid[:, :out_cells] + y[2][:, 2 * lat:2 * lat + out_cells]

    spot = lax.broadcasted_iota(jnp.int32, (1, out_cells), 1) % lat
    full = jnp.where(spot == 0, 0.0, pltpu.roll(total(0), 1, 1))
    full = full + total(1)
    full = full + jnp.where(spot == lat - 1, 0.0, pltpu.roll(total(2), out_cells - 1, 1))
    shift = []
    for g in range(4):
        at = (var_ref[0] - g) & 3
        terms = jnp.zeros((16, 256), jnp.float32)
        for d in range(4):
            terms = jnp.where(at == d, weights[d][9, 0:16, :].astype(jnp.float32), terms)
        shift.append((terms[:, 219:220] + terms[:, 220:221] + terms[:, 221:222])[:6])
    full = full + jnp.concatenate(shift, axis=0)

    rows[...] = jnp.zeros_like(rows)
    for l in range(32):
        col = full[:, l * lat:(l + 1) * lat]
        for g in range(4):
            rows[pl.ds(g * 256 + l, 6, stride=32), :] = col[g * 6:g * 6 + 6]
    turned = rows[...].T
    for g in range(4):
        for h in range(2):
            pairs[pl.ds(g * 2 * lat + h, lat, stride=2), :] = turned[:, g * 256 + h * 128:g * 256 + h * 128 + 128]
    out_ref[...] = pairs[...].astype(out_ref.dtype)


def convolve_inner(var_at, inner, weights):
    _, ch, cells = inner.shape
    smem = pl.BlockSpec(memory_space=pltpu.SMEM)
    vmem = pl.BlockSpec(memory_space=pltpu.VMEM)
    return pl.pallas_call(
        inner_kernel,
        out_shape=jax.ShapeDtypeStruct((216, cells - 128), jnp.float32),
        in_specs=[smem] + [vmem] * 9,
        out_specs=vmem,
        scratch_shapes=[pltpu.VMEM((6, 4 * ch, cells), inner.dtype)],
        cost_estimate=pl.CostEstimate(flops=2 * 512 * 2304 * cells, bytes_accessed=1 << 22, transcendentals=512 * cells),
        compiler_params=pltpu.CompilerParams(vmem_limit_bytes=LIMIT << 20),
    )(var_at, inner, *weights)


def convolve_outer(var_at, inner_taps, inner, outer, weights):
    _, ch, cells = inner.shape
    rest = outer[0].shape[1]
    smem = pl.BlockSpec(memory_space=pltpu.SMEM)
    vmem = pl.BlockSpec(memory_space=pltpu.VMEM)
    return pl.pallas_call(
        outer_kernel,
        out_shape=jax.ShapeDtypeStruct((512, 128), inner.dtype),
        in_specs=[smem] + [vmem] * 14,
        out_specs=vmem,
        scratch_shapes=[
            pltpu.VMEM((6, 4 * ch, rest + 256), inner.dtype),
            pltpu.VMEM((216, cells + rest - 128), jnp.float32),
            pltpu.VMEM((1024, 64), jnp.float32),
            pltpu.VMEM((512, 128), jnp.float32),
        ],
        cost_estimate=pl.CostEstimate(flops=2 * 512 * 2304 * cells, bytes_accessed=1 << 22, transcendentals=512 * cells),
        compiler_params=pltpu.CompilerParams(vmem_limit_bytes=LIMIT << 20),
    )(var_at, inner_taps, inner, *outer, *weights)


def finish_kernel(got_ref, out_ref, pairs):
    pairs[...] = got_ref[...].astype(jnp.float32)
    for k in range(6):
        half, lane = k // 4, k % 4 * 32
        out_ref[k] = jnp.concatenate(
            [pairs[pl.ds(128 * v + half, 64, stride=2), :][:, lane:lane + 32] for v in range(4)], axis=1)


def finish(got):
    vmem = pl.BlockSpec(memory_space=pltpu.VMEM)
    return pl.pallas_call(
        finish_kernel,
        out_shape=jax.ShapeDtypeStruct((6, 64, 128), jnp.float32),
        in_specs=[vmem],
        out_specs=vmem,
        scratch_shapes=[pltpu.VMEM((512, 128), jnp.float32)],
    )(got)


def pack_kernel(core_ref, bias2_ref, first_ref, second_ref, bias1_ref, out_ref):
    half = first_ref.shape[1]
    bf = out_ref.dtype
    at = core_ref[0]
    out_ref[:9] = first_ref[...]
    lane = lax.broadcasted_iota(jnp.int32, (1, 2 * half), 1) % half
    bias2 = jnp.zeros((1, 2 * half), jnp.float32)
    for k in range(bias2_ref.shape[0]):
        bias2 = jnp.where(lane == k, bias2_ref[k], bias2)
    terms = []
    for value in (bias1_ref[...], bias2):
        for _ in range(3):
            term = value.astype(bf).astype(jnp.float32)
            value = value - term
            terms.append(term)
    second = [second_ref[k].astype(jnp.float32) for k in range(9)]
    columns = jnp.concatenate(second + terms + [jnp.zeros((34, 2 * half), jnp.float32)], axis=0).T
    out_ref[9] = jnp.where(at == 0, columns[:half], columns[half:]).astype(bf)


def over_var(parts):
    count = lax.axis_size("var")
    return [parts[0]] + [
        lax.ppermute(parts[d], "var", [(i, (i + d) % count) for i in range(count)]) for d in range(1, count)]


def gathered_weights(conv1_weight, conv1_bias, conv2_weight, conv2_bias):
    smem = pl.BlockSpec(memory_space=pltpu.SMEM)
    taps, channels, inputs = conv1_weight.shape
    mine = pl.pallas_call(
        pack_kernel,
        out_shape=jax.ShapeDtypeStruct((taps + 1, channels // 2, inputs), conv1_weight.dtype),
        grid_spec=pltpu.PrefetchScalarGridSpec(
            num_scalar_prefetch=1,
            grid=(1,),
            in_specs=[
                smem,
                pl.BlockSpec((taps, channels // 2, inputs), lambda i, core: (0, core[0], 0)),
                pl.BlockSpec(conv2_weight.shape, lambda i, core: (0, 0, 0)),
                pl.BlockSpec((1, channels), lambda i, core: (0, 0)),
            ],
            out_specs=pl.BlockSpec((taps + 1, channels // 2, inputs), lambda i, core: (0, 0, 0)),
        ),
    )((lax.axis_index("tile") % 2).reshape(1), conv2_bias, conv1_weight, conv2_weight, conv1_bias.reshape(1, channels))
    return over_var([mine] * 4)


def exchanged_weights(blocks):
    tiles = lax.axis_size("tile")
    return blocks + [lax.ppermute(b, "tile", [(i, i ^ 1) for i in range(tiles)]) for b in blocks]


def body(mesh_latents, edge_idx, edge_weight, conv1_weight, conv1_bias, conv2_weight, conv2_bias):
    tile_at = lax.axis_index("tile")
    tiles = lax.axis_size("tile")
    mesh_dev = mesh_latents.shape[1]
    rim = 64
    core = tile_at % 2
    near = [(i, i ^ 1) for i in range(tiles)]
    far = [(i, (i + 1 if i % 2 else i - 1) % tiles) for i in range(tiles)]
    head, tail = mesh_latents[:, :rim], mesh_latents[:, mesh_dev - rim:]
    near_halo = lax.ppermute(jnp.where(core == 0, tail, head), "tile", near)
    far_halo = lax.ppermute(jnp.where(core == 0, head, tail), "tile", far)
    blocks = gathered_weights(conv1_weight, conv1_bias, conv2_weight, conv2_bias)
    u, wt, lo, hi = prep(edge_idx, edge_weight, tile_at, mesh_dev, mesh_dev * tiles, rim)
    var_at = lax.axis_index("var").reshape(1)
    at = jnp.concatenate([var_at, core.reshape(1)])
    nodes = (at, u, wt, lo, hi, mesh_latents, near_halo, far_halo)
    to_near, to_far = decode("edges", *nodes)
    near_out = lax.ppermute(to_near, "tile", near)
    far_out = lax.ppermute(to_far, "tile", far)
    nodes, _, _ = lax.optimization_barrier((nodes, to_near, to_far))
    inner, = decode("inner", *nodes)
    inner, near_out, far_out = lax.optimization_barrier((inner, near_out, far_out))
    inner = lax.all_to_all(inner, "var", split_axis=0, concat_axis=0, tiled=True)
    outer = decode("outer", *nodes, near_out, far_out)
    outer, blocks = lax.optimization_barrier((outer, blocks))
    weights = exchanged_weights(blocks)
    outer = over_var([None] + list(outer))
    inner_taps = convolve_inner(var_at, inner, weights)
    nodes, near_out, far_out, inner_taps = lax.optimization_barrier((nodes, near_out, far_out, inner_taps))
    outer[0], = decode("own", *nodes, near_out, far_out)
    fields = convolve_outer(var_at, inner_taps, inner, outer, weights)
    got = lax.all_to_all(fields.reshape(256, 2, 128), ("var", "tile"), split_axis=0, concat_axis=0, tiled=True)
    return finish(got.reshape(512, 128)).reshape(6, 1, tiles * 128)


def solution(mesh):
    return jax.shard_map(
        body,
        mesh=mesh,
        in_specs=(
            P("var", "tile"),
            P(None, None, "tile"),
            P(None, None, "tile"),
            P(None, "var", None),
            P("var"),
            P(None, None, "var"),
            P("var"),
        ),
        out_specs=P("var", "tile", None),
        check_vma=False,
    )
```
